1024 devices in a mesh: expert: 32 (over z, y_hi), dp: 32 (over y_lo, x, core).
Axes of the slice: x: 4, y: 8 (y_hi: 2, y_lo: 4; y = y_hi * 4 + y_lo), z: 16, core: 2. Of those that a mesh axis runs over, the one named last changes fastest.
Arguments:
- tokens: bfloat16 [131072, 2560], P(('expert', 'dp')), may hold values from -24 to 24
- cotangent: bfloat16 [131072, 2560], P(('expert', 'dp')), may hold values from -0.09375 to 0.09375
- route_weight: float32 [131072], P(('expert', 'dp')), may hold values from 0.1 to 1
- expert_ids: int32 [131072, 1], P(('expert', 'dp')), may hold values from 0 to 31; in each aligned block of 128 rows (0 to 127, 128 to 255, ...) at most 6 rows name the same one
- dense_gate: bfloat16 [2560, 4096], P('dp', 'expert'), may hold values from -0.125 to 0.125
- dense_up: bfloat16 [2560, 4096], P('dp', 'expert'), may hold values from -0.125 to 0.125
- dense_down_t: bfloat16 [2560, 4096], P('dp', 'expert'), may hold values from -0.5 to 0.5
- seed_map: int32 [32], replicated, may hold values from 0 to 31, as said below
Outputs:
- expert_grads: float32 [32, 2560, 384], P('expert', 'dp')
The draws below stay inside these ranges and needn't reach their ends.
Inputs may be any that keep to these rules, and one draw needn't show every extreme that they name: `expert_ids`: among the 128 tokens of one device no expert is named more than 6 times, a bound that some block reaches. `seed_map`: each expert names one dense slice; several experts may name the same one.
All inputs are finite; a program needn't handle non-finite values.
Results may differ from the reference program's by a relative error of at most 0.0041.
Values may be sent and summed in bfloat16 or wider, within the bound.
No kernel may reach another device: no remote copies, remote signals or barrier semaphores. Data moves between devices by JAX's collectives and lax.ppermute only.
A program may use at most 32 MiB of HBM per device.

```python
import math
import jax
import jax.numpy as jnp
import numpy as np
from jax import lax

D = 2560
H = 128
TOP = 1
TOK_DEV = 128
EXPERTS = 32
SLICES = 32
CAP = 6
TOKENS = 131072
N_EXPERT = 32
N_DP = 32


def draw_seed_map(key, part):
    key = jax.random.fold_in(key, 7)
    offset_key, pick_key = jax.random.split(key)
    offsets = jax.random.randint(offset_key, (EXPERTS,), 0, SLICES, dtype=jnp.int32)
    picked = jax.random.permutation(pick_key, EXPERTS)
    offsets = offsets.at[picked[0]].set(1)
    offsets = offsets.at[picked[1]].set(SLICES - 1)
    offsets = offsets.at[picked[2]].set(SLICES // 2)
    positions = jnp.arange(EXPERTS, dtype=jnp.int32)
    return jnp.mod(positions - offsets, SLICES).astype(jnp.int32)


def strengthened(values, rng, source, target, parts, factor):
    def block_of(position):
        return (jnp.arange(values.shape[position]) // (values.shape[position] // parts)).reshape((-1,) + (1,) * (values.ndim - 1 - position))

    near = jax.random.permutation(rng, parts)[block_of(target)]
    second = (block_of(target) + parts // 2) % parts
    return jnp.where((block_of(source) == near) | (block_of(source) == second), factor * values, values)


def steps_of(stream_key, extent, shards, smallest, top_value):
    factor_of = 1.0
    for axis_at, parts in shards:
        steps = jax.random.uniform(jax.random.fold_in(jax.random.fold_in(stream_key, 6), axis_at), (parts,), jnp.float32, smallest / len(shards), top_value / len(shards))
        factor_of = factor_of * jnp.repeat(jnp.exp(steps), extent[axis_at] // parts).reshape((-1,) + (1,) * (len(extent) - 1 - axis_at))
    return factor_of


def routed_block(rng, own, number, rows, number_of, top, reach, lean):
    sequence = jax.random.permutation(rng, number_of)
    heavy_load, ordinary = load_shares(number_of, rows * top, reach, lean, True), load_shares(number_of, rows * top, reach, lean, False)
    places = jnp.arange(number_of)

    def named(tallies, rotation):
        used = int((tallies > 0).sum())
        fixed = max(1, used // 4)
        passed = fixed + (places - fixed + rotation * (used - fixed)) % max(1, number_of - fixed)
        return jnp.zeros((number_of,), jnp.int32).at[sequence[jnp.where(places < fixed, places, passed)]].set(jnp.asarray(tallies, jnp.int32))

    tallies = jnp.where(number % 4 == 0, named(heavy_load, number // 4), named(ordinary, number - number // 4 - 1))
    mixed = jax.random.permutation(jax.random.fold_in(own, 3), number_of)
    giver, taker = mixed[0:number_of // 2 * 2:2], mixed[1:number_of // 2 * 2:2]
    room = jnp.minimum(tallies[giver] - 1, reach - tallies[taker]) // 2
    room = jnp.where((giver == sequence[0]) | (taker == sequence[0]) | (tallies[taker] == 0), 0, jnp.maximum(room, 0))
    passed = jax.random.randint(jax.random.fold_in(own, 4), (number_of // 2,), 0, 1 << 20) % (room + 1)
    tallies = tallies.at[giver].add(-passed).at[taker].add(passed)
    items = jnp.searchsorted(jnp.cumsum(tallies), jnp.arange(rows * top), side="right").astype(jnp.int32)
    listing = items.reshape(top, rows).T
    listing = listing[jax.random.permutation(jax.random.fold_in(own, 1), rows)]
    rotation = jax.random.randint(jax.random.fold_in(own, 2), (rows, 1), 0, top)
    return jnp.take_along_axis(listing, (jnp.arange(top)[None, :] + rotation) % top, axis=1)


def load_shares(amount, total, bound, skew, full):
    loads = [(1 << 20) // math.isqrt(grade ** skew) + 1 for grade in range(1, amount + 1)]
    largest = bound if full else min(bound, max(-(-total // amount), total * loads[0] // sum(loads)))
    least = 1 if total - largest >= amount - 1 else 0
    holding, surplus = [largest] + [least] * (amount - 1), total - largest - least * (amount - 1)
    while surplus > 0:
        movable = [i for i in range(1, amount) if holding[i] < largest] or [i for i in range(1, amount) if holding[i] < bound]
        pool, remaining = sum([loads[i] for i in movable]), surplus
        for i in movable:
            extra = min(bound - holding[i], max(1, remaining * loads[i] // pool), surplus)
            holding[i] = holding[i] + extra
            surplus = surplus - extra
    return np.array(holding)


def normal_values(stream_key, dims, width, bound, pieces=(), held_as=jnp.bfloat16):
    result = width * jax.random.normal(stream_key, dims, jnp.float32)
    if pieces:
        result = result * steps_of(stream_key, dims, pieces, -0.22, 0.18)
    return jnp.clip(result, -bound, bound).astype(held_as)


def heavy_noise(own_key, extent, spread, most, cuts, heavy, kind=jnp.bfloat16):
    values = spread * jax.random.normal(own_key, extent, jnp.float32)
    if cuts:
        values = values * steps_of(own_key, extent, cuts, -0.22, 0.18)
    return jnp.clip(strengthened(values, jax.random.fold_in(own_key, 3), *heavy), -most, most).astype(kind)


def setup_inputs(seed: int = 0) -> dict:
    seeds = jax.random.split(jax.random.key(seed), 9)
    tokens = heavy_noise(seeds[0], (TOKENS, D), 1.0, 24.0, ((0, 1024),), (0, 1, 512, 6.0))
    cotangent = normal_values(seeds[1], (TOKENS, D), ((TOK_DEV * N_DP) ** -0.5), 0.09375, ((0, 1024),))
    route_weight = jnp.clip(0.1 + 0.9 * jax.random.uniform(seeds[2], (TOKENS,), jnp.float32) ** steps_of(seeds[2], (TOKENS,), ((0, 1024),), -0.2, 0.2), 0.1, 1.0)
    expert_ids_keys = jax.random.split(jax.random.fold_in(seeds[3], 1), TOKENS // TOK_DEV)
    expert_ids_turns = jax.random.permutation(jax.random.fold_in(seeds[3], 3), TOKENS // TOK_DEV)
    expert_ids = jax.vmap(lambda own, number: routed_block(jax.random.fold_in(seeds[3], 2), own, number, TOK_DEV, EXPERTS, TOP, CAP, 2))(expert_ids_keys, expert_ids_turns).reshape((TOKENS, TOP))
    dense_gate = normal_values(seeds[4], (D, SLICES * H), D ** -0.5, 0.125, ((0, 32), (1, 32)))
    dense_up = normal_values(seeds[5], (D, SLICES * H), D ** -0.5, 0.125, ((0, 32), (1, 32)))
    dense_down_t = normal_values(seeds[6], (D, SLICES * H), H ** -0.5, 0.5, ((0, 32), (1, 32)))
    seed_map = draw_seed_map(jax.random.fold_in(seeds[8], 71), 0)
    return dict(tokens=tokens, cotangent=cotangent, route_weight=route_weight, expert_ids=expert_ids, dense_gate=dense_gate, dense_up=dense_up, dense_down_t=dense_down_t, seed_map=seed_map)


def contract_rows(first_operand, second_operand):
    return lax.dot_general(first_operand, second_operand, (((0,), (0,)), ((), ())), preferred_element_type=jnp.float32)


def activation_grads(joined, back_h):
    hidden = back_h.shape[1]
    pre_gate = joined[:, :hidden]
    pre_up = joined[:, hidden:]
    logistic = jax.nn.sigmoid(pre_gate)
    gated = pre_gate * logistic
    gate_slope = logistic * (1.0 + pre_gate * (1.0 - logistic))
    mixed_h = (gated * pre_up).astype(jnp.bfloat16)
    grad_pre = jnp.concatenate([back_h * pre_up * gate_slope, back_h * gated], axis=1).astype(jnp.bfloat16)
    return mixed_h, grad_pre


def weight_terms(row_x, row_g, grad_pre, mixed_h):
    return jnp.concatenate([contract_rows(row_x, grad_pre), contract_rows(row_g, mixed_h)], axis=1)


def expert_term(row_x, row_g, weights):
    hidden = weights.shape[1] // 3
    joined = jnp.dot(row_x, weights[:, :2 * hidden], preferred_element_type=jnp.float32)
    back_h = jnp.dot(row_g, weights[:, 2 * hidden:], preferred_element_type=jnp.float32)
    mixed_h, grad_pre = activation_grads(joined, back_h)
    return weight_terms(row_x, row_g, grad_pre, mixed_h)


def reference(tokens, cotangent, route_weight, expert_ids, dense_gate, dense_up, dense_down_t, seed_map):
    blocks = N_EXPERT * N_DP
    block_ids = expert_ids[:, 0].reshape(blocks, TOK_DEV)
    onehot = (block_ids[:, :, None] == jnp.arange(EXPERTS, dtype=jnp.int32)[None, None, :]).astype(jnp.int32)
    slot_index = jnp.sum(onehot * (jnp.cumsum(onehot, axis=1) - 1), axis=2)
    block_index = jnp.arange(blocks, dtype=jnp.int32)
    source = block_index // N_DP
    data_index = block_index % N_DP
    target = ((block_ids * N_DP + data_index[:, None]) * N_EXPERT + source[:, None]) * CAP + slot_index
    flat_target = target.reshape(-1).astype(jnp.int32)
    total_rows = EXPERTS * N_DP * N_EXPERT * CAP
    routed = (route_weight[:, None] * cotangent.astype(jnp.float32)).astype(jnp.bfloat16)
    buffer_x = jnp.zeros((total_rows, D), jnp.bfloat16).at[flat_target].set(tokens)
    buffer_g = jnp.zeros((total_rows, D), jnp.bfloat16).at[flat_target].set(routed)
    buffer_x = buffer_x.reshape(EXPERTS, N_DP, N_EXPERT * CAP, D)
    buffer_g = buffer_g.reshape(EXPERTS, N_DP, N_EXPERT * CAP, D)

    def one_expert(packed):
        slab_x, slab_g, owner_slice = packed
        first_column = (owner_slice * H).astype(jnp.int32)
        weights = jnp.concatenate([lax.dynamic_slice_in_dim(matrix, first_column, H, 1) for matrix in (dense_gate, dense_up, dense_down_t)], axis=1)

        def one_group(row_pair):
            return expert_term(row_pair[0], row_pair[1], weights)

        group_terms = lax.map(one_group, (slab_x, slab_g))
        return jnp.sum(group_terms, axis=0)

    return lax.map(one_expert, (buffer_x, buffer_g, seed_map))
```

```python
import jax
import jax.numpy as jnp
from jax import lax
from jax.experimental import pallas as pl
from jax.experimental.pallas import tpu as pltpu
from jax.sharding import Mesh
from jax.sharding import PartitionSpec as P

EXPERT = ("zh", "zl", "yh")
DP = ("yl", "x", "c")
SIZES = (4, 4, 2, 4, 4, 2)
DISPATCH = ("yl", "zl", "yh")
PIECES = 4
VMEM_LIMIT = 48 * 1024 * 1024


def iota(shape, dim):
    return lax.broadcasted_iota(jnp.int32, shape, dim)


def place_rows(capacity, ids_ref, weight_ref, tokens_ref, cotangent_ref, out_ref):
    count, features = tokens_ref.shape
    half = features // 2
    total = out_ref.shape[0]
    ids_row = ids_ref[...].reshape(1, count)
    weight_row = weight_ref[...].reshape(1, count)
    row, col = iota((count, count), 0), iota((count, count), 1)
    ids_col = jnp.sum(jnp.where(row == col, ids_row, 0), axis=1, keepdims=True)
    weight_col = jnp.sum(jnp.where(row == col, weight_row, 0.0), axis=1, keepdims=True)
    earlier = (ids_col == ids_row) & (row < col)
    slot = jnp.sum(earlier.astype(jnp.int32), axis=0, keepdims=True)
    base = ids_row * (PIECES * capacity) + slot
    routed = (weight_col * cotangent_ref[...].astype(jnp.float32)).astype(jnp.bfloat16)
    target_row = iota((total, 2 * count), 0)

    def placer(piece):
        codes = jnp.concatenate([base + piece * capacity, base + (piece + 1) * capacity], axis=1)
        return jnp.where(target_row == codes, 1.0, 0.0).astype(jnp.bfloat16)

    rows_x = jnp.concatenate([tokens_ref[:, :half], tokens_ref[:, half:]], axis=0)
    rows_g = jnp.concatenate([routed[:, :half], routed[:, half:]], axis=0)
    out = jnp.dot(placer(0), rows_x, preferred_element_type=jnp.float32)
    out += jnp.dot(placer(2), rows_g, preferred_element_type=jnp.float32)
    out_ref[...] = out.astype(jnp.bfloat16)


def pick_slices(index_ref, stack_ref, out_ref, sems):
    copies = [
        pltpu.make_async_copy(stack_ref.at[index_ref[t]], out_ref.at[t], sems.at[t])
        for t in range(out_ref.shape[0])
    ]
    for copy in copies:
        copy.start()
    for copy in copies:
        copy.wait()


def contract_rows(first, second):
    return lax.dot_general(first, second, (((0,), (0,)), ((), ())), preferred_element_type=jnp.float32)


def expert_grads(
    capacity, core_ref, arrived_ref, own_ref, other_ref, mine_ref, theirs_ref, weights, grads, sems
):
    n_x, n_yl = own_ref.shape[:2]
    total, half = arrived_ref.shape
    rows = total // PIECES
    hidden = weights.shape[-1] // 3
    features = 2 * half
    core = core_ref[0]
    copies = []
    for x in range(n_x):
        copies.append(pltpu.make_async_copy(own_ref.at[x], weights.at[:, x, core], sems.at[x]))
        copies.append(
            pltpu.make_async_copy(other_ref.at[x], weights.at[:, x, 1 - core], sems.at[n_x + x])
        )
    for copy in copies:
        copy.start()
    within, column = iota((rows, total), 0), iota((rows, total), 1)
    source = (within * 10923) >> 16
    first = within + source * ((PIECES - 1) * capacity)
    arrived = arrived_ref[...]

    def sorted_rows(piece):
        chosen = jnp.where(column == first + piece * capacity, 1.0, 0.0).astype(jnp.bfloat16)
        return jnp.dot(chosen, arrived, preferred_element_type=jnp.float32).astype(jnp.bfloat16)

    x0, x1, g0, g1 = (sorted_rows(piece) for piece in range(PIECES))
    for copy in copies:
        copy.wait()
    flat = weights[...].reshape(features, 3 * hidden)

    def product(low, high, lanes):
        return jnp.dot(low, flat[:half, lanes], preferred_element_type=jnp.float32) + jnp.dot(
            high, flat[half:, lanes], preferred_element_type=jnp.float32
        )

    joined = product(x0, x1, slice(0, 2 * hidden))
    back = product(g0, g1, slice(2 * hidden, 3 * hidden))
    pre_gate, pre_up = joined[:, :hidden], joined[:, hidden:]
    logistic = jax.nn.sigmoid(pre_gate)
    gated = pre_gate * logistic
    slope = logistic * (1.0 + pre_gate * (1.0 - logistic))
    mixed = (gated * pre_up).astype(jnp.bfloat16)
    grad_pre = jnp.concatenate([back * pre_up * slope, back * gated], axis=1).astype(jnp.bfloat16)
    n_half = n_yl // 2
    blocks = (n_half, n_x, 2, weights.shape[3])
    for part, (rows_x, rows_g) in enumerate(((x0, g0), (x1, g1))):
        at = slice(part * n_half, (part + 1) * n_half)
        grads[at, :, :, :, : 2 * hidden] = contract_rows(rows_x, grad_pre).reshape(
            blocks + (2 * hidden,)
        )
        grads[at, :, :, :, 2 * hidden :] = contract_rows(rows_g, mixed).reshape(blocks + (hidden,))
    for x in range(n_x):
        mine_ref[x] = grads[:, x, core]
        theirs_ref[x] = grads[:, x, 1 - core].astype(jnp.bfloat16)


def on_device(
    tokens, cotangent, route_weight, expert_ids, dense_gate, dense_up, dense_down_t, seed_map
):
    n_zh, n_zl, n_yh, n_yl, n_x, n_c = SIZES
    experts = n_zh * n_zl * n_yh
    count, features = tokens.shape
    capacity = 3 * count // (2 * experts)
    half = features // 2
    block, hidden = dense_gate.shape
    width = 3 * hidden
    chunk = PIECES * capacity
    vmem = pl.BlockSpec(memory_space=pltpu.VMEM)
    smem = pl.BlockSpec(memory_space=pltpu.SMEM)
    anywhere = pl.BlockSpec(memory_space=pl.ANY)
    params = pltpu.CompilerParams(vmem_limit_bytes=VMEM_LIMIT)
    bf16 = jnp.bfloat16

    placed = pl.pallas_call(
        lambda *refs: place_rows(capacity, *refs),
        out_shape=jax.ShapeDtypeStruct((experts * chunk, half), bf16),
        in_specs=[vmem] * 4,
        out_specs=vmem,
        compiler_params=params,
        name="place_rows",
    )(expert_ids[:, 0], route_weight, tokens, cotangent)
    arrived = lax.all_to_all(
        placed.reshape(experts, chunk, half), DISPATCH, split_axis=0, concat_axis=0, tiled=True
    ).reshape(experts * chunk, half)

    zl, zh = lax.axis_index("zl"), lax.axis_index("zh")
    core = lax.axis_index("c")
    own = jnp.concatenate([dense_gate, dense_up, dense_down_t], axis=1)
    slices = lax.all_gather(own, ("zh", "zl"), axis=0, tiled=False)
    seeds = lax.dynamic_index_in_dim(seed_map.reshape(n_zh, n_zl, n_yh), zl, 1, keepdims=False).T
    offered = pl.pallas_call(
        pick_slices,
        out_shape=jax.ShapeDtypeStruct((n_yh * n_yl, block, width), bf16),
        in_specs=[smem, anywhere],
        out_specs=anywhere,
        scratch_shapes=[pltpu.SemaphoreType.DMA((n_yh * n_yl,))],
        compiler_params=params,
        name="pick_slices",
    )((seeds // n_yh).reshape(-1), slices)
    sent = lax.all_to_all(offered, ("yh", "yl"), split_axis=0, concat_axis=0, tiled=True)
    my_seed = seeds[lax.axis_index("yh"), lax.axis_index("yl")]
    seeded = lax.dynamic_slice_in_dim(sent, (my_seed % n_yh) * n_yl, n_yl, 0)
    own_rows = lax.all_gather(seeded, "x", axis=0, tiled=False)
    swap = [(i, 1 - i) for i in range(n_c)]
    other_rows = lax.ppermute(own_rows, "c", swap)

    half_shape = (n_x, n_yl, block, width)
    mine, theirs = pl.pallas_call(
        lambda *refs: expert_grads(capacity, *refs),
        out_shape=[
            jax.ShapeDtypeStruct(half_shape, jnp.float32),
            jax.ShapeDtypeStruct(half_shape, bf16),
        ],
        in_specs=[smem, vmem, anywhere, anywhere],
        out_specs=[vmem, vmem],
        scratch_shapes=[
            pltpu.VMEM((n_yl, n_x, n_c, block, width), bf16),
            pltpu.VMEM((n_yl, n_x, n_c, block, width), jnp.float32),
            pltpu.SemaphoreType.DMA((2 * n_x,)),
        ],
        compiler_params=params,
        name="expert_grads",
    )(core.reshape(1), arrived, own_rows, other_rows)
    pair = (mine + lax.ppermute(theirs, "c", swap).astype(jnp.float32)).astype(bf16)
    by_x = lax.all_to_all(pair, "x", split_axis=0, concat_axis=0, tiled=True)
    row_sums = jnp.sum(by_x.astype(jnp.float32), axis=0).astype(bf16)
    total = None
    for step in range(n_yl):
        part = lax.dynamic_index_in_dim(row_sums, (zh + step) % n_yl, 0, keepdims=False)
        moves = [
            (a * n_yl + b, b * n_yl + (a + step) % n_yl) for a in range(n_zh) for b in range(n_yl)
        ]
        got = lax.ppermute(part, ("zh", "yl"), moves).astype(jnp.float32)
        total = got if total is None else total + got
    return total[None]


def solution(mesh):
    fine = Mesh(mesh.devices.reshape(SIZES), EXPERT + DP)
    rows = P(EXPERT + DP, None)
    dense = P(DP, EXPERT)
    return jax.shard_map(
        on_device,
        mesh=fine,
        in_specs=(rows, rows, P(EXPERT + DP), rows, dense, dense, dense, P()),
        out_specs=P(EXPERT, DP, None),
        check_vma=False,
    )
```

```python
import jax
import jax.numpy as jnp
from jax import lax
from jax.experimental import pallas as pl
from jax.experimental.pallas import tpu as pltpu
from jax.sharding import Mesh
from jax.sharding import PartitionSpec as P

EXPERT = ("zh", "zl", "yh")
DP = ("yl", "x", "c")
SIZES = (4, 4, 2, 4, 4, 2)
DISPATCH = ("yl", "zl", "yh")
PIECES = 4
VMEM_LIMIT = 48 * 1024 * 1024


def iota(shape, dim):
    return lax.broadcasted_iota(jnp.int32, shape, dim)


def place_rows(capacity, ids_ref, weight_ref, tokens_ref, cotangent_ref, out_ref):
    count, features = tokens_ref.shape
    half = features // 2
    total = out_ref.shape[0]
    ids_row = ids_ref[...].reshape(1, count)
    weight_row = weight_ref[...].reshape(1, count)
    row, col = iota((count, count), 0), iota((count, count), 1)
    ids_col = jnp.sum(jnp.where(row == col, ids_row, 0), axis=1, keepdims=True)
    weight_col = jnp.sum(jnp.where(row == col, weight_row, 0.0), axis=1, keepdims=True)
    earlier = (ids_col == ids_row) & (row < col)
    slot = jnp.sum(earlier.astype(jnp.int32), axis=0, keepdims=True)
    base = ids_row * (PIECES * capacity) + slot
    routed = (weight_col * cotangent_ref[...].astype(jnp.float32)).astype(jnp.bfloat16)
    target_row = iota((total, 2 * count), 0)

    def placer(piece):
        codes = jnp.concatenate([base + piece * capacity, base + (piece + 1) * capacity], axis=1)
        return jnp.where(target_row == codes, 1.0, 0.0).astype(jnp.bfloat16)

    rows_x = jnp.concatenate([tokens_ref[:, :half], tokens_ref[:, half:]], axis=0)
    rows_g = jnp.concatenate([routed[:, :half], routed[:, half:]], axis=0)
    out = jnp.dot(placer(0), rows_x, preferred_element_type=jnp.float32)
    out += jnp.dot(placer(2), rows_g, preferred_element_type=jnp.float32)
    out_ref[...] = out.astype(jnp.bfloat16)


def pick_slices(zl_ref, seeds_ref, stack_ref, out_ref, sems):
    _, n_zl, n_yh, n_yl, _, _ = SIZES
    copies = []
    for yh in range(n_yh):
        for yl in range(n_yl):
            seed = seeds_ref[(yl * n_zl + zl_ref[0]) * n_yh + yh]
            to = yh * n_yl + yl
            copies.append(
                pltpu.make_async_copy(stack_ref.at[seed // n_yh], out_ref.at[to], sems.at[to])
            )
    for copy in copies:
        copy.start()
    for copy in copies:
        copy.wait()


def contract_rows(first, second):
    return lax.dot_general(first, second, (((0,), (0,)), ((), ())), preferred_element_type=jnp.float32)


def expert_grads(
    capacity, core_ref, arrived_ref, own_ref, other_ref, mine_ref, theirs_ref, weights, grads, sems
):
    n_x, n_yl = own_ref.shape[:2]
    total, half = arrived_ref.shape
    rows = total // PIECES
    hidden = weights.shape[-1] // 3
    features = 2 * half
    core = core_ref[0]
    copies = []
    for x in range(n_x):
        copies.append(pltpu.make_async_copy(own_ref.at[x], weights.at[:, x, core], sems.at[x]))
        copies.append(
            pltpu.make_async_copy(other_ref.at[x], weights.at[:, x, 1 - core], sems.at[n_x + x])
        )
    for copy in copies:
        copy.start()
    within, column = iota((rows, total), 0), iota((rows, total), 1)
    source = (within * 10923) >> 16
    first = within + source * ((PIECES - 1) * capacity)
    arrived = arrived_ref[...]

    def sorted_rows(piece):
        chosen = jnp.where(column == first + piece * capacity, 1.0, 0.0).astype(jnp.bfloat16)
        return jnp.dot(chosen, arrived, preferred_element_type=jnp.float32).astype(jnp.bfloat16)

    x0, x1, g0, g1 = (sorted_rows(piece) for piece in range(PIECES))
    for copy in copies:
        copy.wait()
    flat = weights[...].reshape(features, 3 * hidden)

    def product(low, high, lanes):
        return jnp.dot(low, flat[:half, lanes], preferred_element_type=jnp.float32) + jnp.dot(
            high, flat[half:, lanes], preferred_element_type=jnp.float32
        )

    joined = product(x0, x1, slice(0, 2 * hidden))
    back = product(g0, g1, slice(2 * hidden, 3 * hidden))
    pre_gate, pre_up = joined[:, :hidden], joined[:, hidden:]
    logistic = jax.nn.sigmoid(pre_gate)
    gated = pre_gate * logistic
    slope = logistic * (1.0 + pre_gate * (1.0 - logistic))
    mixed = (gated * pre_up).astype(jnp.bfloat16)
    grad_pre = jnp.concatenate([back * pre_up * slope, back * gated], axis=1).astype(jnp.bfloat16)
    n_half = n_yl // 2
    blocks = (n_half, n_x, 2, weights.shape[3])
    for part, (rows_x, rows_g) in enumerate(((x0, g0), (x1, g1))):
        at = slice(part * n_half, (part + 1) * n_half)
        grads[at, :, :, :, : 2 * hidden] = contract_rows(rows_x, grad_pre).reshape(
            blocks + (2 * hidden,)
        )
        grads[at, :, :, :, 2 * hidden :] = contract_rows(rows_g, mixed).reshape(blocks + (hidden,))
    for x in range(n_x):
        mine_ref[x] = grads[:, x, core]
        theirs_ref[x] = grads[:, x, 1 - core].astype(jnp.bfloat16)


def on_device(
    tokens, cotangent, route_weight, expert_ids, dense_gate, dense_up, dense_down_t, seed_map
):
    n_zh, n_zl, n_yh, n_yl, n_x, n_c = SIZES
    experts = n_zh * n_zl * n_yh
    count, features = tokens.shape
    capacity = 3 * count // (2 * experts)
    half = features // 2
    block, hidden = dense_gate.shape
    width = 3 * hidden
    chunk = PIECES * capacity
    vmem = pl.BlockSpec(memory_space=pltpu.VMEM)
    smem = pl.BlockSpec(memory_space=pltpu.SMEM)
    anywhere = pl.BlockSpec(memory_space=pl.ANY)
    params = pltpu.CompilerParams(vmem_limit_bytes=VMEM_LIMIT)
    bf16 = jnp.bfloat16

    placed = pl.pallas_call(
        lambda *refs: place_rows(capacity, *refs),
        out_shape=jax.ShapeDtypeStruct((experts * chunk, half), bf16),
        in_specs=[vmem] * 4,
        out_specs=vmem,
        compiler_params=params,
        name="place_rows",
    )(expert_ids[:, 0], route_weight, tokens, cotangent)
    arrived = lax.all_to_all(
        placed.reshape(experts, chunk, half), DISPATCH, split_axis=0, concat_axis=0, tiled=True
    ).reshape(experts * chunk, half)

    zl, core = lax.axis_index("zl"), lax.axis_index("c")
    own = jnp.concatenate([dense_gate, dense_up, dense_down_t], axis=1)
    slices = lax.all_gather(own, ("zh", "zl"), axis=0, tiled=False)
    offered = pl.pallas_call(
        pick_slices,
        out_shape=jax.ShapeDtypeStruct((n_yh * n_yl, block, width), bf16),
        in_specs=[smem, smem, anywhere],
        out_specs=anywhere,
        scratch_shapes=[pltpu.SemaphoreType.DMA((n_yh * n_yl,))],
        compiler_params=params,
        name="pick_slices",
    )(zl.reshape(1), seed_map, slices)
    sent = lax.all_to_all(offered, ("yh", "yl"), split_axis=0, concat_axis=0, tiled=True)
    my_seed = seed_map[lax.axis_index(DISPATCH)]
    seeded = lax.dynamic_slice_in_dim(sent, (my_seed % n_yh) * n_yl, n_yl, 0)
    own_rows = lax.all_gather(seeded, "x", axis=0, tiled=False)
    swap = [(i, 1 - i) for i in range(n_c)]
    other_rows = lax.ppermute(own_rows, "c", swap)

    half_shape = (n_x, n_yl, block, width)
    mine, theirs = pl.pallas_call(
        lambda *refs: expert_grads(capacity, *refs),
        out_shape=[
            jax.ShapeDtypeStruct(half_shape, jnp.float32),
            jax.ShapeDtypeStruct(half_shape, bf16),
        ],
        in_specs=[smem, vmem, anywhere, anywhere],
        out_specs=[vmem, vmem],
        scratch_shapes=[
            pltpu.VMEM((n_yl, n_x, n_c, block, width), bf16),
            pltpu.VMEM((n_yl, n_x, n_c, block, width), jnp.float32),
            pltpu.SemaphoreType.DMA((2 * n_x,)),
        ],
        compiler_params=params,
        name="expert_grads",
    )(core.reshape(1), arrived, own_rows, other_rows)
    pair = (mine + lax.ppermute(theirs, "c", swap).astype(jnp.float32)).astype(bf16)
    by_x = lax.all_to_all(pair, "x", split_axis=0, concat_axis=0, tiled=True)
    row_sums = jnp.sum(by_x.astype(jnp.float32), axis=0).astype(bf16)
    by_home = lax.all_to_all(row_sums, "yl", split_axis=0, concat_axis=0, tiled=True)
    by_group = lax.all_to_all(by_home, "zh", split_axis=0, concat_axis=0, tiled=True)
    total = jnp.sum(by_group.astype(jnp.float32), axis=0)
    return total[None]


def solution(mesh):
    fine = Mesh(mesh.devices.reshape(SIZES), EXPERT + DP)
    rows = P(EXPERT + DP, None)
    dense = P(DP, EXPERT)
    return jax.shard_map(
        on_device,
        mesh=fine,
        in_specs=(rows, rows, P(EXPERT + DP), rows, dense, dense, dense, P()),
        out_specs=P(EXPERT, DP, None),
        check_vma=False,
    )
```

```python
import jax
import jax.numpy as jnp
from jax import lax
from jax.experimental import pallas as pl
from jax.experimental.pallas import tpu as pltpu
from jax.sharding import Mesh
from jax.sharding import PartitionSpec as P

EXPERT = ("zh", "zl", "yh")
DP = ("yl", "x", "c")
SIZES = (4, 4, 2, 4, 4, 2)
DISPATCH = ("yl", "zl", "yh")
PIECES = 4
VMEM_LIMIT = 48 * 1024 * 1024


def iota(shape, dim):
    return lax.broadcasted_iota(jnp.int32, shape, dim)


def place_rows(capacity, ids_ref, weight_ref, tokens_ref, cotangent_ref, out_ref):
    count, features = tokens_ref.shape
    half = features // 2
    total = out_ref.shape[0]
    ids_row = ids_ref[...].reshape(1, count)
    weight_row = weight_ref[...].reshape(1, count)
    row, col = iota((count, count), 0), iota((count, count), 1)
    ids_col = jnp.sum(jnp.where(row == col, ids_row, 0), axis=1, keepdims=True)
    weight_col = jnp.sum(jnp.where(row == col, weight_row, 0.0), axis=1, keepdims=True)
    earlier = (ids_col == ids_row) & (row < col)
    slot = jnp.sum(earlier.astype(jnp.int32), axis=0, keepdims=True)
    base = ids_row * (PIECES * capacity) + slot
    routed = (weight_col * cotangent_ref[...].astype(jnp.float32)).astype(jnp.bfloat16)
    target_row = iota((total, 2 * count), 0)

    def placer(piece):
        codes = jnp.concatenate([base + piece * capacity, base + (piece + 1) * capacity], axis=1)
        return jnp.where(target_row == codes, 1.0, 0.0).astype(jnp.bfloat16)

    rows_x = jnp.concatenate([tokens_ref[:, :half], tokens_ref[:, half:]], axis=0)
    rows_g = jnp.concatenate([routed[:, :half], routed[:, half:]], axis=0)
    out = jnp.dot(placer(0), rows_x, preferred_element_type=jnp.float32)
    out += jnp.dot(placer(2), rows_g, preferred_element_type=jnp.float32)
    out_ref[...] = out.astype(jnp.bfloat16)


def pick_slices(zl_ref, seeds_ref, stack_ref, out_ref, sems):
    _, n_zl, n_yh, n_yl, _, _ = SIZES
    copies = []
    for yh in range(n_yh):
        for yl in range(n_yl):
            seed = seeds_ref[(yl * n_zl + zl_ref[0]) * n_yh + yh]
            to = yh * n_yl + yl
            copies.append(
                pltpu.make_async_copy(stack_ref.at[seed // n_yh], out_ref.at[to], sems.at[to])
            )
    for copy in copies:
        copy.start()
    for copy in copies:
        copy.wait()


def contract_rows(first, second):
    return lax.dot_general(first, second, (((0,), (0,)), ((), ())), preferred_element_type=jnp.float32)


def expert_grads(
    capacity, core_ref, arrived_ref, own_ref, other_ref, mine_ref, theirs_ref, weights, grads
):
    n_x, n_yl = own_ref.shape[:2]
    total, half = arrived_ref.shape
    rows = total // PIECES
    hidden = weights.shape[-1] // 3
    features = 2 * half
    core = core_ref[0]
    for x in range(n_x):
        weights[:, x, core] = own_ref[x]
        weights[:, x, 1 - core] = other_ref[x]
    within, column = iota((rows, total), 0), iota((rows, total), 1)
    source = (within * 10923) >> 16
    first = within + source * ((PIECES - 1) * capacity)
    arrived = arrived_ref[...]

    def sorted_rows(piece):
        chosen = jnp.where(column == first + piece * capacity, 1.0, 0.0).astype(jnp.bfloat16)
        return jnp.dot(chosen, arrived, preferred_element_type=jnp.float32).astype(jnp.bfloat16)

    x0, x1, g0, g1 = (sorted_rows(piece) for piece in range(PIECES))
    flat = weights[...].reshape(features, 3 * hidden)

    def product(low, high, lanes):
        return jnp.dot(low, flat[:half, lanes], preferred_element_type=jnp.float32) + jnp.dot(
            high, flat[half:, lanes], preferred_element_type=jnp.float32
        )

    joined = product(x0, x1, slice(0, 2 * hidden))
    back = product(g0, g1, slice(2 * hidden, 3 * hidden))
    pre_gate, pre_up = joined[:, :hidden], joined[:, hidden:]
    logistic = jax.nn.sigmoid(pre_gate)
    gated = pre_gate * logistic
    slope = logistic * (1.0 + pre_gate * (1.0 - logistic))
    mixed = (gated * pre_up).astype(jnp.bfloat16)
    grad_pre = jnp.concatenate([back * pre_up * slope, back * gated], axis=1).astype(jnp.bfloat16)
    n_half = n_yl // 2
    blocks = (n_half, n_x, 2, weights.shape[3])
    for part, (rows_x, rows_g) in enumerate(((x0, g0), (x1, g1))):
        at = slice(part * n_half, (part + 1) * n_half)
        grads[at, :, :, :, : 2 * hidden] = contract_rows(rows_x, grad_pre).reshape(
            blocks + (2 * hidden,)
        )
        grads[at, :, :, :, 2 * hidden :] = contract_rows(rows_g, mixed).reshape(blocks + (hidden,))
    for x in range(n_x):
        mine_ref[x] = grads[:, x, core]
        theirs_ref[x] = grads[:, x, 1 - core].astype(jnp.bfloat16)


def on_device(
    tokens, cotangent, route_weight, expert_ids, dense_gate, dense_up, dense_down_t, seed_map
):
    n_zh, n_zl, n_yh, n_yl, n_x, n_c = SIZES
    experts = n_zh * n_zl * n_yh
    count, features = tokens.shape
    capacity = 3 * count // (2 * experts)
    half = features // 2
    block, hidden = dense_gate.shape
    width = 3 * hidden
    chunk = PIECES * capacity
    vmem = pl.BlockSpec(memory_space=pltpu.VMEM)
    smem = pl.BlockSpec(memory_space=pltpu.SMEM)
    anywhere = pl.BlockSpec(memory_space=pl.ANY)
    params = pltpu.CompilerParams(vmem_limit_bytes=VMEM_LIMIT)
    bf16 = jnp.bfloat16

    placed = pl.pallas_call(
        lambda *refs: place_rows(capacity, *refs),
        out_shape=jax.ShapeDtypeStruct((experts * chunk, half), bf16),
        in_specs=[vmem] * 4,
        out_specs=vmem,
        compiler_params=params,
        name="place_rows",
    )(expert_ids[:, 0], route_weight, tokens, cotangent)
    arrived = lax.all_to_all(
        placed.reshape(experts, chunk, half), DISPATCH, split_axis=0, concat_axis=0, tiled=True
    ).reshape(experts * chunk, half)

    zl, core = lax.axis_index("zl"), lax.axis_index("c")
    own = jnp.concatenate([dense_gate, dense_up, dense_down_t], axis=1)
    slices = lax.all_gather(own, ("zh", "zl"), axis=0, tiled=False)
    offered = pl.pallas_call(
        pick_slices,
        out_shape=jax.ShapeDtypeStruct((n_yh * n_yl, block, width), bf16),
        in_specs=[smem, smem, anywhere],
        out_specs=anywhere,
        scratch_shapes=[pltpu.SemaphoreType.DMA((n_yh * n_yl,))],
        compiler_params=params,
        name="pick_slices",
    )(zl.reshape(1), seed_map, slices)
    sent = lax.all_to_all(offered, ("yh", "yl"), split_axis=0, concat_axis=0, tiled=True)
    my_seed = seed_map[lax.axis_index(DISPATCH)]
    seeded = lax.dynamic_slice_in_dim(sent, (my_seed % n_yh) * n_yl, n_yl, 0)
    own_rows = lax.all_gather(seeded, "x", axis=0, tiled=False)
    swap = [(i, 1 - i) for i in range(n_c)]
    other_rows = lax.ppermute(own_rows, "c", swap)

    half_shape = (n_x, n_yl, block, width)
    mine, theirs = pl.pallas_call(
        lambda *refs: expert_grads(capacity, *refs),
        out_shape=[
            jax.ShapeDtypeStruct(half_shape, jnp.float32),
            jax.ShapeDtypeStruct(half_shape, bf16),
        ],
        in_specs=[smem, vmem, vmem, vmem],
        out_specs=[vmem, vmem],
        scratch_shapes=[
            pltpu.VMEM((n_yl, n_x, n_c, block, width), bf16),
            pltpu.VMEM((n_yl, n_x, n_c, block, width), jnp.float32),
        ],
        compiler_params=params,
        name="expert_grads",
    )(core.reshape(1), arrived, own_rows, other_rows)
    pair = (mine + lax.ppermute(theirs, "c", swap).astype(jnp.float32)).astype(bf16)
    by_x = lax.all_to_all(pair, "x", split_axis=0, concat_axis=0, tiled=True)
    row_sums = jnp.sum(by_x.astype(jnp.float32), axis=0).astype(bf16)
    by_home = lax.all_to_all(row_sums, "yl", split_axis=0, concat_axis=0, tiled=True)
    by_group = lax.all_to_all(by_home, "zh", split_axis=0, concat_axis=0, tiled=True)
    total = jnp.sum(by_group.astype(jnp.float32), axis=0)
    return total[None]


def solution(mesh):
    fine = Mesh(mesh.devices.reshape(SIZES), EXPERT + DP)
    rows = P(EXPERT + DP, None)
    dense = P(DP, EXPERT)
    return jax.shard_map(
        on_device,
        mesh=fine,
        in_specs=(rows, rows, P(EXPERT + DP), rows, dense, dense, dense, P()),
        out_specs=P(EXPERT, DP, None),
        check_vma=False,
    )
```

```python
import jax
import jax.numpy as jnp
from jax import lax
from jax.experimental import pallas as pl
from jax.experimental.pallas import tpu as pltpu
from jax.sharding import Mesh
from jax.sharding import PartitionSpec as P

EXPERT = ("zh", "zl", "yh")
DP = ("yl", "x", "c")
SIZES = (4, 4, 2, 4, 4, 2)
DISPATCH = ("yl", "zl", "yh")
PIECES = 4
VMEM_LIMIT = 24 * 1024 * 1024


def iota(shape, dim):
    return lax.broadcasted_iota(jnp.int32, shape, dim)


def place_rows(capacity, ids_ref, weight_ref, tokens_ref, cotangent_ref, out_ref):
    count, features = tokens_ref.shape
    half = features // 2
    total = out_ref.shape[0]
    ids_row = ids_ref[...].reshape(1, count)
    weight_row = weight_ref[...].reshape(1, count)
    row, col = iota((count, count), 0), iota((count, count), 1)
    ids_col = jnp.sum(jnp.where(row == col, ids_row, 0), axis=1, keepdims=True)
    weight_col = jnp.sum(jnp.where(row == col, weight_row, 0.0), axis=1, keepdims=True)
    earlier = (ids_col == ids_row) & (row < col)
    slot = jnp.sum(earlier.astype(jnp.int32), axis=0, keepdims=True)
    base = ids_row * (PIECES * capacity) + slot
    routed = (weight_col * cotangent_ref[...].astype(jnp.float32)).astype(jnp.bfloat16)
    target_row = iota((total, 2 * count), 0)

    def placer(piece):
        codes = jnp.concatenate([base + piece * capacity, base + (piece + 1) * capacity], axis=1)
        return jnp.where(target_row == codes, 1.0, 0.0).astype(jnp.bfloat16)

    rows_x = jnp.concatenate([tokens_ref[:, :half], tokens_ref[:, half:]], axis=0)
    rows_g = jnp.concatenate([routed[:, :half], routed[:, half:]], axis=0)
    out = jnp.dot(placer(0), rows_x, preferred_element_type=jnp.float32)
    out += jnp.dot(placer(2), rows_g, preferred_element_type=jnp.float32)
    out_ref[...] = out.astype(jnp.bfloat16)


def pick_slices(zl_ref, seeds_ref, stack_ref, out_ref, sems):
    _, n_zl, n_yh, n_yl, _, _ = SIZES
    copies = []
    for yh in range(n_yh):
        for yl in range(n_yl):
            seed = seeds_ref[(yl * n_zl + zl_ref[0]) * n_yh + yh]
            to = yh * n_yl + yl
            copies.append(
                pltpu.make_async_copy(stack_ref.at[seed // n_yh], out_ref.at[to], sems.at[to])
            )
    for copy in copies:
        copy.start()
    for copy in copies:
        copy.wait()


def contract_rows(first, second):
    return lax.dot_general(first, second, (((0,), (0,)), ((), ())), preferred_element_type=jnp.float32)


def expert_grads(
    capacity, core_ref, arrived_ref, own_ref, other_ref, mine_ref, theirs_ref, weights
):
    n_x, n_yl = own_ref.shape[:2]
    total, half = arrived_ref.shape
    rows = total // PIECES
    hidden = weights.shape[-1] // 3
    features = 2 * half
    core = core_ref[0]
    for x in range(n_x):
        weights[:, x, core] = own_ref[x]
        weights[:, x, 1 - core] = other_ref[x]
    within, column = iota((rows, total), 0), iota((rows, total), 1)
    source = (within * 10923) >> 16
    first = within + source * ((PIECES - 1) * capacity)
    arrived = arrived_ref[...]

    def sorted_rows(piece):
        chosen = jnp.where(column == first + piece * capacity, 1.0, 0.0).astype(jnp.bfloat16)
        return jnp.dot(chosen, arrived, preferred_element_type=jnp.float32).astype(jnp.bfloat16)

    x0, x1, g0, g1 = (sorted_rows(piece) for piece in range(PIECES))
    flat = weights[...].reshape(features, 3 * hidden)

    def product(low, high, lanes):
        return jnp.dot(low, flat[:half, lanes], preferred_element_type=jnp.float32) + jnp.dot(
            high, flat[half:, lanes], preferred_element_type=jnp.float32
        )

    joined = product(x0, x1, slice(0, 2 * hidden))
    back = product(g0, g1, slice(2 * hidden, 3 * hidden))
    pre_gate, pre_up = joined[:, :hidden], joined[:, hidden:]
    logistic = jax.nn.sigmoid(pre_gate)
    gated = pre_gate * logistic
    slope = logistic * (1.0 + pre_gate * (1.0 - logistic))
    mixed = (gated * pre_up).astype(jnp.bfloat16)
    grad_pre = jnp.concatenate([back * pre_up * slope, back * gated], axis=1).astype(jnp.bfloat16)
    n_half = n_yl // 2
    blocks = (n_half, n_x, 2, weights.shape[3])
    for part, (rows_x, rows_g) in enumerate(((x0, g0), (x1, g1))):
        from_x = contract_rows(rows_x, grad_pre).reshape(blocks + (2 * hidden,))
        from_g = contract_rows(rows_g, mixed).reshape(blocks + (hidden,))
        both = jnp.concatenate([from_x, from_g], axis=-1)
        for yl in range(n_half):
            for x in range(n_x):
                first, second = both[yl, x, 0], both[yl, x, 1]
                to = (x, part * n_half + yl)
                mine_ref[to] = jnp.where(core == 0, first, second)
                theirs_ref[to] = jnp.where(core == 0, second, first).astype(jnp.bfloat16)


def on_device(
    tokens, cotangent, route_weight, expert_ids, dense_gate, dense_up, dense_down_t, seed_map
):
    n_zh, n_zl, n_yh, n_yl, n_x, n_c = SIZES
    experts = n_zh * n_zl * n_yh
    count, features = tokens.shape
    capacity = 3 * count // (2 * experts)
    half = features // 2
    block, hidden = dense_gate.shape
    width = 3 * hidden
    chunk = PIECES * capacity
    vmem = pl.BlockSpec(memory_space=pltpu.VMEM)
    smem = pl.BlockSpec(memory_space=pltpu.SMEM)
    anywhere = pl.BlockSpec(memory_space=pl.ANY)
    params = pltpu.CompilerParams(vmem_limit_bytes=VMEM_LIMIT)
    bf16 = jnp.bfloat16

    placed = pl.pallas_call(
        lambda *refs: place_rows(capacity, *refs),
        out_shape=jax.ShapeDtypeStruct((experts * chunk, half), bf16),
        in_specs=[vmem] * 4,
        out_specs=vmem,
        compiler_params=params,
        name="place_rows",
    )(expert_ids[:, 0], route_weight, tokens, cotangent)
    arrived = lax.all_to_all(
        placed.reshape(experts, chunk, half), DISPATCH, split_axis=0, concat_axis=0, tiled=True
    ).reshape(experts * chunk, half)

    zl, core = lax.axis_index("zl"), lax.axis_index("c")
    own = jnp.concatenate([dense_gate, dense_up, dense_down_t], axis=1)
    slices = lax.all_gather(own, ("zh", "zl"), axis=0, tiled=False)
    offered = pl.pallas_call(
        pick_slices,
        out_shape=jax.ShapeDtypeStruct((n_yh * n_yl, block, width), bf16),
        in_specs=[smem, smem, anywhere],
        out_specs=anywhere,
        scratch_shapes=[pltpu.SemaphoreType.DMA((n_yh * n_yl,))],
        compiler_params=params,
        name="pick_slices",
    )(zl.reshape(1), seed_map, slices)
    sent = lax.all_to_all(offered, ("yh", "yl"), split_axis=0, concat_axis=0, tiled=True)
    my_seed = seed_map[lax.axis_index(DISPATCH)]
    seeded = lax.dynamic_slice_in_dim(sent, (my_seed % n_yh) * n_yl, n_yl, 0)
    own_rows = lax.all_gather(seeded, "x", axis=0, tiled=False)
    swap = [(i, 1 - i) for i in range(n_c)]
    other_rows = lax.ppermute(own_rows, "c", swap)

    half_shape = (n_x, n_yl, block, width)
    mine, theirs = pl.pallas_call(
        lambda *refs: expert_grads(capacity, *refs),
        out_shape=[
            jax.ShapeDtypeStruct(half_shape, jnp.float32),
            jax.ShapeDtypeStruct(half_shape, bf16),
        ],
        in_specs=[smem, vmem, vmem, vmem],
        out_specs=[vmem, vmem],
        scratch_shapes=[
            pltpu.VMEM((n_yl, n_x, n_c, block, width), bf16),
        ],
        compiler_params=params,
        name="expert_grads",
    )(core.reshape(1), arrived, own_rows, other_rows)
    pair = (mine + lax.ppermute(theirs, "c", swap).astype(jnp.float32)).astype(bf16)
    by_x = lax.all_to_all(pair, "x", split_axis=0, concat_axis=0, tiled=True)
    row_sums = jnp.sum(by_x.astype(jnp.float32), axis=0).astype(bf16)
    by_home = lax.all_to_all(row_sums, "yl", split_axis=0, concat_axis=0, tiled=True)
    by_group = lax.all_to_all(by_home, "zh", split_axis=0, concat_axis=0, tiled=True)
    total = jnp.sum(by_group.astype(jnp.float32), axis=0)
    return total[None]


def solution(mesh):
    fine = Mesh(mesh.devices.reshape(SIZES), EXPERT + DP)
    rows = P(EXPERT + DP, None)
    dense = P(DP, EXPERT)
    return jax.shard_map(
        on_device,
        mesh=fine,
        in_specs=(rows, rows, P(EXPERT + DP), rows, dense, dense, dense, P()),
        out_specs=P(EXPERT, DP, None),
        check_vma=False,
    )
```

```python
import jax
import jax.numpy as jnp
from jax import lax
from jax.experimental import pallas as pl
from jax.experimental.pallas import tpu as pltpu
from jax.sharding import Mesh
from jax.sharding import PartitionSpec as P

EXPERT = ("zh", "zl", "yh")
DP = ("yl", "x", "c")
SIZES = (4, 4, 2, 4, 4, 2)
DISPATCH = ("yl", "zl", "yh")
PIECES = 4
VMEM_LIMIT = 16 * 1024 * 1024


def iota(shape, dim):
    return lax.broadcasted_iota(jnp.int32, shape, dim)


def place_rows(capacity, ids_ref, weight_ref, tokens_ref, cotangent_ref, out_ref):
    count, features = tokens_ref.shape
    half = features // 2
    total = out_ref.shape[0]
    ids_row = ids_ref[...].reshape(1, count)
    weight_row = weight_ref[...].reshape(1, count)
    row, col = iota((count, count), 0), iota((count, count), 1)
    ids_col = jnp.sum(jnp.where(row == col, ids_row, 0), axis=1, keepdims=True)
    weight_col = jnp.sum(jnp.where(row == col, weight_row, 0.0), axis=1, keepdims=True)
    earlier = (ids_col == ids_row) & (row < col)
    slot = jnp.sum(earlier.astype(jnp.int32), axis=0, keepdims=True)
    base = ids_row * (PIECES * capacity) + slot
    routed = (weight_col * cotangent_ref[...].astype(jnp.float32)).astype(jnp.bfloat16)
    target_row = iota((total, 2 * count), 0)

    def placer(piece):
        codes = jnp.concatenate([base + piece * capacity, base + (piece + 1) * capacity], axis=1)
        return jnp.where(target_row == codes, 1.0, 0.0).astype(jnp.bfloat16)

    rows_x = jnp.concatenate([tokens_ref[:, :half], tokens_ref[:, half:]], axis=0)
    rows_g = jnp.concatenate([routed[:, :half], routed[:, half:]], axis=0)
    out = jnp.dot(placer(0), rows_x, preferred_element_type=jnp.float32)
    out += jnp.dot(placer(2), rows_g, preferred_element_type=jnp.float32)
    out_ref[...] = out.astype(jnp.bfloat16)


def pick_slices(seed_map_ref, stack_ref, out_ref, seeds_ref, sem):
    _, n_zl, n_yh, n_yl, _, _ = SIZES
    zl = lax.axis_index("zl")
    copy = pltpu.make_async_copy(seed_map_ref, seeds_ref, sem)
    copy.start()
    copy.wait()
    for yh in range(n_yh):
        for yl in range(n_yl):
            seed = seeds_ref[(yl * n_zl + zl) * n_yh + yh]
            out_ref[yh * n_yl + yl] = stack_ref[seed // n_yh]


def contract_rows(first, second):
    return lax.dot_general(first, second, (((0,), (0,)), ((), ())), preferred_element_type=jnp.float32)


def expert_grads(
    capacity, core_ref, arrived_ref, own_ref, other_ref, mine_ref, theirs_ref, weights
):
    n_x, n_yl = own_ref.shape[:2]
    total, half = arrived_ref.shape
    rows = total // PIECES
    hidden = weights.shape[-1] // 3
    features = 2 * half
    core = core_ref[0]
    for x in range(n_x):
        weights[:, x, core] = own_ref[x]
        weights[:, x, 1 - core] = other_ref[x]
    within, column = iota((rows, total), 0), iota((rows, total), 1)
    source = (within * 10923) >> 16
    first = within + source * ((PIECES - 1) * capacity)
    arrived = arrived_ref[...]

    def sorted_rows(piece):
        chosen = jnp.where(column == first + piece * capacity, 1.0, 0.0).astype(jnp.bfloat16)
        return jnp.dot(chosen, arrived, preferred_element_type=jnp.float32).astype(jnp.bfloat16)

    x0, x1, g0, g1 = (sorted_rows(piece) for piece in range(PIECES))
    flat = weights[...].reshape(features, 3 * hidden)

    def product(low, high, lanes):
        return jnp.dot(low, flat[:half, lanes], preferred_element_type=jnp.float32) + jnp.dot(
            high, flat[half:, lanes], preferred_element_type=jnp.float32
        )

    joined = product(x0, x1, slice(0, 2 * hidden))
    back = product(g0, g1, slice(2 * hidden, 3 * hidden))
    pre_gate, pre_up = joined[:, :hidden], joined[:, hidden:]
    logistic = jax.nn.sigmoid(pre_gate)
    gated = pre_gate * logistic
    slope = logistic * (1.0 + pre_gate * (1.0 - logistic))
    mixed = (gated * pre_up).astype(jnp.bfloat16)
    grad_pre = jnp.concatenate([back * pre_up * slope, back * gated], axis=1).astype(jnp.bfloat16)
    n_half = n_yl // 2
    blocks = (n_half, n_x, 2, weights.shape[3])
    for part, (rows_x, rows_g) in enumerate(((x0, g0), (x1, g1))):
        from_x = contract_rows(rows_x, grad_pre).reshape(blocks + (2 * hidden,))
        from_g = contract_rows(rows_g, mixed).reshape(blocks + (hidden,))
        both = jnp.concatenate([from_x, from_g], axis=-1)
        for yl in range(n_half):
            for x in range(n_x):
                first, second = both[yl, x, 0], both[yl, x, 1]
                to = (x, part * n_half + yl)
                mine_ref[to] = jnp.where(core == 0, first, second)
                theirs_ref[to] = jnp.where(core == 0, second, first).astype(jnp.bfloat16)


def on_device(
    tokens, cotangent, route_weight, expert_ids, dense_gate, dense_up, dense_down_t, seed_map
):
    n_zh, n_zl, n_yh, n_yl, n_x, n_c = SIZES
    experts = n_zh * n_zl * n_yh
    count, features = tokens.shape
    capacity = 3 * count // (2 * experts)
    half = features // 2
    block, hidden = dense_gate.shape
    width = 3 * hidden
    chunk = PIECES * capacity
    vmem = pl.BlockSpec(memory_space=pltpu.VMEM)
    smem = pl.BlockSpec(memory_space=pltpu.SMEM)
    params = pltpu.CompilerParams(vmem_limit_bytes=VMEM_LIMIT)
    bf16 = jnp.bfloat16

    placed = pl.pallas_call(
        lambda *refs: place_rows(capacity, *refs),
        out_shape=jax.ShapeDtypeStruct((experts * chunk, half), bf16),
        in_specs=[vmem] * 4,
        out_specs=vmem,
        compiler_params=params,
        name="place_rows",
    )(expert_ids[:, 0], route_weight, tokens, cotangent)
    arrived = lax.all_to_all(
        placed.reshape(experts, chunk, half), DISPATCH, split_axis=0, concat_axis=0, tiled=True
    ).reshape(experts * chunk, half)

    core = lax.axis_index("c")
    own = jnp.concatenate([dense_gate, dense_up, dense_down_t], axis=1)
    slices = lax.all_gather(own, ("zh", "zl"), axis=0, tiled=False)
    offered = pl.pallas_call(
        pick_slices,
        out_shape=jax.ShapeDtypeStruct((n_yh * n_yl, block, width), bf16),
        in_specs=[pl.BlockSpec(memory_space=pl.ANY), vmem],
        out_specs=vmem,
        scratch_shapes=[pltpu.SMEM(seed_map.shape, jnp.int32), pltpu.SemaphoreType.DMA],
        compiler_params=params,
        name="pick_slices",
    )(seed_map, slices)
    sent = lax.all_to_all(offered, ("yh", "yl"), split_axis=0, concat_axis=0, tiled=True)
    my_seed = seed_map[lax.axis_index(DISPATCH)]
    seeded = lax.dynamic_slice_in_dim(sent, (my_seed % n_yh) * n_yl, n_yl, 0)
    own_rows = lax.all_gather(seeded, "x", axis=0, tiled=False)
    swap = [(i, 1 - i) for i in range(n_c)]
    other_rows = lax.ppermute(own_rows, "c", swap)

    half_shape = (n_x, n_yl, block, width)
    mine, theirs = pl.pallas_call(
        lambda *refs: expert_grads(capacity, *refs),
        out_shape=[
            jax.ShapeDtypeStruct(half_shape, jnp.float32),
            jax.ShapeDtypeStruct(half_shape, bf16),
        ],
        in_specs=[smem, vmem, vmem, vmem],
        out_specs=[vmem, vmem],
        scratch_shapes=[
            pltpu.VMEM((n_yl, n_x, n_c, block, width), bf16),
        ],
        compiler_params=params,
        name="expert_grads",
    )(core.reshape(1), arrived, own_rows, other_rows)
    pair = (mine + lax.ppermute(theirs, "c", swap).astype(jnp.float32)).astype(bf16)
    by_x = lax.all_to_all(pair, "x", split_axis=0, concat_axis=0, tiled=True)
    row_sums = jnp.sum(by_x.astype(jnp.float32), axis=0).astype(bf16)
    by_home = lax.all_to_all(row_sums, "yl", split_axis=0, concat_axis=0, tiled=True)
    by_group = lax.all_to_all(by_home, "zh", split_axis=0, concat_axis=0, tiled=True)
    total = jnp.sum(by_group.astype(jnp.float32), axis=0)
    return total[None]


def solution(mesh):
    fine = Mesh(mesh.devices.reshape(SIZES), EXPERT + DP)
    rows = P(EXPERT + DP, None)
    dense = P(DP, EXPERT)
    return jax.shard_map(
        on_device,
        mesh=fine,
        in_specs=(rows, rows, P(EXPERT + DP), rows, dense, dense, dense, P()),
        out_specs=P(EXPERT, DP, None),
        check_vma=False,
    )
```
